32 devices in a mesh: seq: 8 (over z, x), kvh: 4 (over y, core).
Axes of the slice: x: 2, y: 2, z: 4, core: 2. Of those that a mesh axis runs over, the one named last changes fastest.
Arguments:
- queries: bfloat16 [4096, 4, 4, 128], P('seq', 'kvh'), may hold values from -12 to 12
- key_states: bfloat16 [4096, 4, 128], P('seq', 'kvh'), may hold values from -10 to 10
- value_states: bfloat16 [4096, 4, 128], P('seq', 'kvh'), may hold values from -4 to 4
- grad_out: bfloat16 [4096, 4, 4, 128], P('seq', 'kvh'), may hold values from -96 to 96
- ancestors: int32 [8, 6], replicated, may hold values from -1 to 6, as said below
- query_weight: bfloat16 [8192, 4, 4, 128], P(None, 'kvh'), may hold values from -0.0625 to 0.0625
- key_weight: bfloat16 [8192, 4, 128], P(None, 'kvh'), may hold values from -0.0625 to 0.0625
- value_weight: bfloat16 [8192, 4, 128], P(None, 'kvh'), may hold values from -0.0625 to 0.0625
Outputs:
- grad_input: bfloat16 [4096, 8192], P(('seq', 'kvh'))
- grad_key: bfloat16 [4096, 4, 128], P('seq', 'kvh')
- grad_value: bfloat16 [4096, 4, 128], P('seq', 'kvh')
The draws below stay inside these ranges and needn't reach their ends.
Inputs may be any that keep to these rules, and one draw needn't show every extreme that they name: Row b lists the strict ancestor blocks of block b, the root block 0 in slot 0 and one level deeper in each further slot, all below b; the remaining slots hold -1. Block 0 has no ancestors and is an ancestor of every other block; the blocks of every subtree are consecutive; some block has 6 ancestors.
All inputs are finite; a program needn't handle non-finite values.
Results may differ from the reference program's by a relative error of at most 0.015.
Values may be sent and summed in bfloat16 or wider, within the bound.
A program may use at most 128 MiB of HBM per device.

```python
from functools import partial
import jax
import jax.numpy as jnp
from jax import lax

MODEL = 8192
HEAD_DIM = 128
Q_PER_KV = 4
KV_HEADS = 4
BLOCK = 512
DEPTH = 6
TOKENS = 4096
BLOCKS = 8


def draw_queries(key, part):
    values = jax.random.normal(jax.random.fold_in(key, 11), (TOKENS, KV_HEADS, Q_PER_KV, HEAD_DIM), jnp.float32)
    values = jnp.clip(values, -4.0, 4.0)
    return values.astype(jnp.bfloat16)


def draw_key_states(key, part):
    values = jax.random.normal(jax.random.fold_in(key, 13), (TOKENS, KV_HEADS, HEAD_DIM), jnp.float32)
    values = jnp.clip(values, -4.0, 4.0)
    return values.astype(jnp.bfloat16)


def draw_ancestors(key, part):
    chain_start = jax.random.randint(jax.random.fold_in(key, 3), (), 1, BLOCKS - DEPTH + 1).astype(jnp.int32)
    coins = jax.random.randint(jax.random.fold_in(key, 5), (BLOCKS,), 0, 2)
    picks = jax.random.randint(jax.random.fold_in(key, 7), (BLOCKS,), 0, 1 << 20)
    level_index = jnp.arange(DEPTH + 1, dtype=jnp.int32)

    def advance(carried, block_id):
        path_now, depth_now = carried
        deepest = jnp.minimum(depth_now, DEPTH - 1)
        forced = (block_id >= chain_start) & (block_id < chain_start + DEPTH)
        free_pick = jnp.where(coins[block_id] == 1, deepest, picks[block_id] % (deepest + 1))
        chosen = jnp.where(forced, block_id - chain_start, free_pick)
        kept = jnp.where(level_index <= chosen, path_now, -1)
        next_path = jnp.where(level_index == chosen + 1, block_id, kept)
        return ((next_path.astype(jnp.int32), (chosen + 1).astype(jnp.int32)), kept[:DEPTH].astype(jnp.int32))
    start_path = jnp.full((DEPTH + 1,), -1, jnp.int32).at[0].set(0)
    carried = (start_path, jnp.zeros((), jnp.int32))
    carried, rows_out = lax.scan(advance, carried, jnp.arange(1, BLOCKS, dtype=jnp.int32))
    first_row = jnp.full((1, DEPTH), -1, jnp.int32)
    return jnp.concatenate([first_row, rows_out], 0)


def block_scale(rng, extent, cuts, least, top_value):
    def one(axis_at, parts):
        heights = jax.random.uniform(jax.random.fold_in(jax.random.fold_in(rng, 6), axis_at), (parts,), jnp.float32, least / len(cuts), top_value / len(cuts))
        return jnp.repeat(jnp.exp(heights), extent[axis_at] // parts).reshape((-1,) + (1,) * (len(extent) - axis_at - 1))

    loudness = one(*cuts[0])
    for cut in cuts[1:]:
        loudness = loudness * one(*cut)
    return loudness


def centred(key, dims, deviation, most, pieces=(), kind=jnp.bfloat16):
    gain = block_scale(key, dims, pieces, -0.22, 0.18) if pieces else 1.0
    result = jax.random.normal(key, dims, jnp.float32) * deviation * gain
    return jnp.minimum(jnp.maximum(result, -most), most).astype(kind)


def setup_inputs(seed: int = 0) -> dict:
    key_of = jax.random.split(jax.random.key(seed), 9)
    return {
        "queries": draw_queries(jax.random.fold_in(key_of[8], 71), 0),
        "key_states": draw_key_states(jax.random.fold_in(key_of[8], 71), 0),
        "value_states": centred(key_of[2], (TOKENS, KV_HEADS, HEAD_DIM), 1.0, 4.0, ((0, 8), (1, 4))),
        "grad_out": centred(key_of[3], (TOKENS, KV_HEADS, Q_PER_KV, HEAD_DIM), 16.0, 96.0, ((0, 8), (1, 4))),
        "ancestors": draw_ancestors(jax.random.fold_in(key_of[8], 71), 0),
        "query_weight": centred(key_of[5], (MODEL, KV_HEADS, Q_PER_KV, HEAD_DIM), MODEL ** -0.5, 0.0625, ((1, 4),)),
        "key_weight": centred(key_of[6], (MODEL, KV_HEADS, HEAD_DIM), MODEL ** -0.5, 0.0625, ((1, 4),)),
        "value_weight": centred(key_of[7], (MODEL, KV_HEADS, HEAD_DIM), MODEL ** -0.5, 0.0625, ((1, 4),)),
    }


def rounded(values):
    return lax.optimization_barrier(values.astype(jnp.bfloat16)).astype(jnp.float32)


def take_rows(source, row_base):
    return lax.dynamic_slice_in_dim(source, row_base, BLOCK, 0)


def block_terms(query_block, grad_block, key_rows, value_rows, visible):
    factor = HEAD_DIM ** -0.5
    query_wide = query_block.astype(jnp.float32)
    grad_wide = grad_block.astype(jnp.float32)
    key_wide = key_rows.astype(jnp.float32)
    value_wide = value_rows.astype(jnp.float32)
    scores = jnp.einsum("qgd,kd->gqk", query_wide, key_wide) * factor
    scores = jnp.where(visible[None], scores, -jnp.inf)
    row_peak = jnp.max(scores, axis=-1, keepdims=True)
    exp_terms = jnp.where(visible[None], jnp.exp(scores - row_peak), 0.0)
    attn_weight = exp_terms / jnp.sum(exp_terms, axis=-1, keepdims=True)
    grad_probs = jnp.einsum("qgd,kd->gqk", grad_wide, value_wide)
    delta_row = jnp.sum(attn_weight * grad_probs, axis=-1, keepdims=True)
    prob_low = rounded(attn_weight)
    grad_scores = rounded(attn_weight * (grad_probs - delta_row) * factor)
    query_term = jnp.einsum("gqk,kd->qgd", grad_scores, key_wide)
    key_term = jnp.einsum("gqk,qgd->kd", grad_scores, query_wide)
    value_term = jnp.einsum("gqk,qgd->kd", prob_low, grad_wide)
    return query_term, key_term, value_term


def reference(queries, key_states, value_states, grad_out, ancestors, query_weight, key_weight, value_weight):
    offsets = jnp.arange(BLOCK, dtype=jnp.int32)
    causal = offsets[:, None] >= offsets[None, :]
    input_total = jnp.zeros((TOKENS, MODEL), jnp.float32)
    key_grads = []
    value_grads = []
    for head_id in range(KV_HEADS):
        head_queries = queries[:, head_id]
        head_grads = grad_out[:, head_id]
        head_keys = key_states[:, head_id]
        head_values = value_states[:, head_id]

        def one_block(block_id):
            block_start = (block_id * BLOCK).astype(jnp.int32)
            listed = lax.dynamic_index_in_dim(ancestors, block_id, 0, keepdims=False)
            starts = (jnp.maximum(listed, 0) * BLOCK).astype(jnp.int32)
            all_starts = jnp.concatenate([starts, block_start[None]])
            key_rows = jax.vmap(partial(take_rows, head_keys))(all_starts).reshape((DEPTH + 1) * BLOCK, HEAD_DIM)
            value_rows = jax.vmap(partial(take_rows, head_values))(all_starts).reshape((DEPTH + 1) * BLOCK, HEAD_DIM)
            ancestor_mask = jnp.broadcast_to(jnp.repeat(listed >= 0, BLOCK)[None, :], (BLOCK, DEPTH * BLOCK))
            visible = jnp.concatenate([ancestor_mask, causal], 1)
            query_block = take_rows(head_queries, block_start)
            grad_block = take_rows(head_grads, block_start)
            query_term, key_term, value_term = block_terms(query_block, grad_block, key_rows, value_rows, visible)
            positions = (all_starts[:, None] + offsets[None, :]).reshape(-1).astype(jnp.int32)
            return query_term, key_term, value_term, positions

        query_terms, key_terms, value_terms, positions = lax.map(one_block, jnp.arange(BLOCKS, dtype=jnp.int32))
        flat_positions = positions.reshape(-1)
        key_total = jnp.zeros((TOKENS, HEAD_DIM), jnp.float32).at[flat_positions].add(key_terms.reshape(-1, HEAD_DIM))
        value_total = jnp.zeros((TOKENS, HEAD_DIM), jnp.float32).at[flat_positions].add(value_terms.reshape(-1, HEAD_DIM))
        query_low = query_terms.reshape(TOKENS, Q_PER_KV * HEAD_DIM).astype(jnp.bfloat16)
        key_low = key_total.astype(jnp.bfloat16)
        value_low = value_total.astype(jnp.bfloat16)
        head_term = jnp.dot(query_low, query_weight[:, head_id].reshape(MODEL, Q_PER_KV * HEAD_DIM).T, preferred_element_type=jnp.float32)
        head_term = head_term + jnp.dot(key_low, key_weight[:, head_id].T, preferred_element_type=jnp.float32)
        head_term = head_term + jnp.dot(value_low, value_weight[:, head_id].T, preferred_element_type=jnp.float32)
        input_total = input_total + rounded(head_term)
        key_grads.append(key_low)
        value_grads.append(value_low)
    return input_total.astype(jnp.bfloat16), jnp.stack(key_grads, 1), jnp.stack(value_grads, 1)
```

```python
import functools

import jax
import jax.numpy as jnp
from jax import lax
from jax.experimental import pallas as pl
from jax.experimental.pallas import tpu as pltpu
from jax.sharding import PartitionSpec as P

BLOCK = 512
WIDTH = 128
HEADS = 4
NT = (((1,), (1,)), ((), ()))
NN = (((1,), (0,)), ((), ()))
TN = (((0,), (0,)), ((), ()))
LOG2E = 1.4426950408889634


def dot(a, b, dims):
    return lax.dot_general(a, b, dims, preferred_element_type=jnp.float32)


def causal_mask():
    keys = lax.broadcasted_iota(jnp.int32, (BLOCK, BLOCK), 0)
    rows = lax.broadcasted_iota(jnp.int32, (BLOCK, BLOCK), 1)
    return keys <= rows


def attention_kernel(vis_ref, q_ref, do_ref, kv_ref, dq_ref, dkv_ref, dq_acc, peak, mass, weighted):
    me = lax.axis_index("seq")
    blocks = kv_ref.shape[0] // BLOCK
    factor = WIDTH ** -0.5

    def rows_of(j):
        return pl.ds(pl.multiple_of(j * BLOCK, BLOCK), BLOCK)

    def stats(j, first):
        keys = kv_ref[rows_of(j), :WIDTH]
        values = kv_ref[rows_of(j), WIDTH:]
        for g in range(HEADS):
            lanes = slice(g * WIDTH, (g + 1) * WIDTH)
            scores = dot(keys, q_ref[:, lanes], NT) * (factor * LOG2E)
            if first:
                scores = jnp.where(causal_mask(), scores, -jnp.inf)
            grads = dot(values, do_ref[:, lanes], NT)
            top = jnp.max(scores, axis=0, keepdims=True)
            if not first:
                old = peak[g]
                top = jnp.maximum(top, old)
            terms = jnp.exp2(scores - top)
            total = jnp.sum(terms, axis=0, keepdims=True)
            moved = jnp.sum(terms * grads, axis=0, keepdims=True)
            if not first:
                scale = jnp.exp2(old - top)
                total = total + mass[g] * scale
                moved = moved + weighted[g] * scale
            peak[g] = top
            mass[g] = total
            weighted[g] = moved

    def backward(j, first):
        keys = kv_ref[rows_of(j), :WIDTH]
        values = kv_ref[rows_of(j), WIDTH:]
        key_grad = jnp.zeros((BLOCK, WIDTH), jnp.float32)
        value_grad = jnp.zeros((BLOCK, WIDTH), jnp.float32)
        for g in range(HEADS):
            lanes = slice(g * WIDTH, (g + 1) * WIDTH)
            q = q_ref[:, lanes]
            do = do_ref[:, lanes]
            scores = dot(keys, q, NT) * (factor * LOG2E)
            probs = jnp.exp2(scores - peak[g])
            if first:
                probs = jnp.where(causal_mask(), probs, 0.0)
            grads = dot(values, do, NT)
            dscores = (probs * ((grads - weighted[g]) * factor)).astype(jnp.bfloat16)
            value_grad = value_grad + dot(probs.astype(jnp.bfloat16), do, NN)
            key_grad = key_grad + dot(dscores, q, NN)
            term = dot(dscores, keys, TN)
            if first:
                dq_acc[:, lanes] = term
            else:
                dq_acc[:, lanes] += term
        dkv_ref[rows_of(j), :WIDTH] = key_grad.astype(jnp.bfloat16)
        dkv_ref[rows_of(j), WIDTH:] = value_grad.astype(jnp.bfloat16)

    stats(me, True)

    def stats_step(j, carry):
        @pl.when(vis_ref[j] > 0)
        def _():
            stats(j, False)

        return carry

    lax.fori_loop(0, me, stats_step, 0)
    for g in range(HEADS):
        weighted[g] = weighted[g] / mass[g]
        peak[g] = peak[g] + jnp.log2(mass[g])
    backward(me, True)

    def grad_step(j, carry):
        seen = (vis_ref[j] > 0) & (j < me)

        @pl.when(seen)
        def _():
            backward(j, False)

        @pl.when(jnp.logical_not(seen) & (j != me))
        def _():
            dkv_ref[rows_of(j), :] = jnp.zeros((BLOCK, 2 * WIDTH), jnp.bfloat16)

        return carry

    lax.fori_loop(0, blocks, grad_step, 0)
    dq_ref[...] = dq_acc[...].astype(jnp.bfloat16)


def attention(visible, q, do, kv):
    window = kv.shape[0]
    vmem = pl.BlockSpec(memory_space=pltpu.VMEM)
    pairs = HEADS * BLOCK * BLOCK * 7
    return pl.pallas_call(
        attention_kernel,
        out_shape=(
            jax.ShapeDtypeStruct((BLOCK, HEADS * WIDTH), jnp.bfloat16),
            jax.ShapeDtypeStruct((window, 2 * WIDTH), jnp.bfloat16),
        ),
        in_specs=[pl.BlockSpec(memory_space=pltpu.SMEM), vmem, vmem, vmem],
        out_specs=(vmem, vmem),
        scratch_shapes=[
            pltpu.VMEM((BLOCK, HEADS * WIDTH), jnp.float32),
            pltpu.VMEM((HEADS, 1, BLOCK), jnp.float32),
            pltpu.VMEM((HEADS, 1, BLOCK), jnp.float32),
            pltpu.VMEM((HEADS, 1, BLOCK), jnp.float32),
        ],
        compiler_params=pltpu.CompilerParams(vmem_limit_bytes=48 * 2**20),
        cost_estimate=pl.CostEstimate(
            flops=7 * 2 * pairs * WIDTH, bytes_accessed=6 * 2**20, transcendentals=2 * pairs
        ),
        name="attention",
    )(visible, q, do, kv)


def project_kernel(
    size, chunks, dq_ref, dkv_ref, wq_ref, wk_ref, wv_ref, out_ref,
    rows_all, weights, product, own, core_out, core_in, far_out, far_in,
    w_sem, core_send, core_recv, far_send, far_recv,
):
    me = lax.axis_index("kvh")
    layer = me // 2
    core = me % 2
    layers = size // 2
    rows = BLOCK // size
    width = wq_ref.shape[0] // chunks
    qw = HEADS * WIDTH
    peer = layer * 2 + 1 - core

    def weight_copies(i):
        at = pl.ds(pl.multiple_of(i * width, width), width)
        return [
            pltpu.make_async_copy(wq_ref.at[at, :], weights.at[i, :, pl.ds(0, qw)], w_sem.at[i, 0]),
            pltpu.make_async_copy(wk_ref.at[at, :], weights.at[i, :, pl.ds(qw, WIDTH)], w_sem.at[i, 1]),
            pltpu.make_async_copy(
                wv_ref.at[at, :], weights.at[i, :, pl.ds(qw + WIDTH, WIDTH)], w_sem.at[i, 2]
            ),
        ]

    def start_weights(i, carry):
        for copy in weight_copies(i):
            copy.start()
        return carry

    lax.fori_loop(0, chunks, start_weights, 0)
    barrier = pltpu.get_barrier_semaphore()
    far = [lax.rem(layer + d, layers) for d in range(layers)]
    pl.semaphore_signal(barrier, inc=1, device_id={"kvh": peer}, device_id_type=pl.DeviceIdType.MESH)
    for d in range(1, layers):
        pl.semaphore_signal(
            barrier, inc=1, device_id={"kvh": far[d] * 2 + core}, device_id_type=pl.DeviceIdType.MESH
        )
    rows_all[:, :qw] = dq_ref[...]
    rows_all[:, qw:] = dkv_ref[...]
    pl.semaphore_wait(barrier, layers)

    def core_copy(d, i):
        return pltpu.make_async_remote_copy(
            core_out.at[d, i], core_in.at[d, i], core_send.at[d, i], core_recv.at[d, i],
            device_id={"kvh": peer}, device_id_type=pl.DeviceIdType.MESH,
        )

    def far_copy(d, i):
        return pltpu.make_async_remote_copy(
            far_out.at[d - 1, i], far_in.at[d - 1, i], far_send.at[d - 1, i], far_recv.at[d - 1, i],
            device_id={"kvh": far[d] * 2 + core}, device_id_type=pl.DeviceIdType.MESH,
        )

    def part(d, which):
        return pl.ds(pl.multiple_of((far[d] * 2 + which) * rows, rows), rows)

    def begin(i):
        for copy in weight_copies(i):
            copy.wait()
        slot = i % 2
        product[slot] = dot(rows_all[...], weights[i], NT)
        for d in list(range(1, layers)) + [0]:
            core_out[d, i] = product[slot, part(d, 1 - core), :].astype(jnp.bfloat16)
            core_copy(d, i).start()

    def forward(i):
        slot = i % 2
        for d in range(1, layers):
            core_copy(d, i).wait_recv()
            far_out[d - 1, i] = (
                product[slot, part(d, core), :] + core_in[d, i].astype(jnp.float32)
            ).astype(jnp.bfloat16)
            far_copy(d, i).start()
        own[i] = product[slot, part(0, core), :]

    begin(0)

    def step(i, carry):
        begin(i)
        forward(i - 1)
        return carry

    lax.fori_loop(1, chunks, step, 0)
    forward(chunks - 1)

    def finish(i, carry):
        core_copy(0, i).wait_recv()
        total = own[i] + core_in[0, i].astype(jnp.float32)
        for d in range(1, layers):
            far_copy(d, i).wait_recv()
            total = total + far_in[d - 1, i].astype(jnp.float32)
        out_ref[:, pl.ds(pl.multiple_of(i * width, width), width)] = total.astype(jnp.bfloat16)
        for d in range(layers):
            core_copy(d, i).wait_send()
        for d in range(1, layers):
            far_copy(d, i).wait_send()
        return carry

    lax.fori_loop(0, chunks, finish, 0)


def project(size, dq, dkv, wq, wk, wv):
    model = wq.shape[0]
    rows = BLOCK // size
    layers = size // 2
    chunks = 16
    width = model // chunks
    vmem = pl.BlockSpec(memory_space=pltpu.VMEM)
    hbm = pl.BlockSpec(memory_space=pl.ANY)
    full = (HEADS + 2) * WIDTH
    return pl.pallas_call(
        functools.partial(project_kernel, size, chunks),
        out_shape=jax.ShapeDtypeStruct((rows, model), jnp.bfloat16),
        in_specs=[vmem, vmem, hbm, hbm, hbm],
        out_specs=vmem,
        scratch_shapes=[
            pltpu.VMEM((BLOCK, full), jnp.bfloat16),
            pltpu.VMEM((chunks, width, full), jnp.bfloat16),
            pltpu.VMEM((2, BLOCK, width), jnp.float32),
            pltpu.VMEM((chunks, rows, width), jnp.float32),
            pltpu.VMEM((layers, chunks, rows, width), jnp.bfloat16),
            pltpu.VMEM((layers, chunks, rows, width), jnp.bfloat16),
            pltpu.VMEM((layers - 1, chunks, rows, width), jnp.bfloat16),
            pltpu.VMEM((layers - 1, chunks, rows, width), jnp.bfloat16),
            pltpu.SemaphoreType.DMA((chunks, 3)),
            pltpu.SemaphoreType.DMA((layers, chunks)),
            pltpu.SemaphoreType.DMA((layers, chunks)),
            pltpu.SemaphoreType.DMA((layers - 1, chunks)),
            pltpu.SemaphoreType.DMA((layers - 1, chunks)),
        ],
        compiler_params=pltpu.CompilerParams(
            collective_id=1, has_side_effects=True, vmem_limit_bytes=56 * 2**20
        ),
        cost_estimate=pl.CostEstimate(
            flops=2 * BLOCK * full * model, bytes_accessed=2 * full * model, transcendentals=0
        ),
        name="project",
    )(dq, dkv, wq, wk, wv)


def local(
    size, queries, key_states, value_states, grad_out, ancestors, query_weight, key_weight, value_weight
):
    model = query_weight.shape[0]
    q = queries.reshape(BLOCK, HEADS * WIDTH)
    do = grad_out.reshape(BLOCK, HEADS * WIDTH)
    kv = jnp.concatenate([key_states[:, 0], value_states[:, 0]], 1)
    gathered = lax.all_gather(kv, "seq", axis=0, tiled=True)
    blocks = ancestors.shape[0]
    me = lax.axis_index("seq")
    listed = lax.dynamic_index_in_dim(ancestors, me, 0, keepdims=False)
    ids = jnp.arange(blocks, dtype=jnp.int32)
    visible = jnp.any(listed[None, :] == ids[:, None], axis=1).astype(jnp.int32)
    dq, dkv = attention(visible, q, do, gathered)
    pair = lax.psum_scatter(dkv, "seq", scatter_dimension=0, tiled=True)
    grad_input = project(
        size, dq, pair,
        query_weight.reshape(model, HEADS * WIDTH), key_weight[:, 0], value_weight[:, 0],
    )
    return (grad_input, pair[:, None, :WIDTH], pair[:, None, WIDTH:])


def solution(mesh):
    return jax.shard_map(
        functools.partial(local, mesh.shape["kvh"]),
        mesh=mesh,
        in_specs=(
            P("seq", "kvh", None, None),
            P("seq", "kvh", None),
            P("seq", "kvh", None),
            P("seq", "kvh", None, None),
            P(),
            P(None, "kvh", None, None),
            P(None, "kvh", None),
            P(None, "kvh", None),
        ),
        out_specs=(P(("seq", "kvh"), None), P("seq", "kvh", None), P("seq", "kvh", None)),
        check_vma=False,
    )
```

```python
import functools

import jax
import jax.numpy as jnp
from jax import lax
from jax.experimental import pallas as pl
from jax.experimental.pallas import tpu as pltpu
from jax.sharding import PartitionSpec as P

BLOCK = 512
WIDTH = 128
HEADS = 4
NT = (((1,), (1,)), ((), ()))
NN = (((1,), (0,)), ((), ()))
TN = (((0,), (0,)), ((), ()))
LOG2E = 1.4426950408889634


def dot(a, b, dims):
    return lax.dot_general(a, b, dims, preferred_element_type=jnp.float32)


def causal_mask():
    keys = lax.broadcasted_iota(jnp.int32, (BLOCK, BLOCK), 0)
    rows = lax.broadcasted_iota(jnp.int32, (BLOCK, BLOCK), 1)
    return keys <= rows


def attention_kernel(
    columns, bias_ref, q_ref, do_ref, kv_ref, dq_ref, dkv_ref,
    kv_all, dq_acc, peak, mass, weighted, col, peer_out, peer_in, up_in, up_out,
    got, z_sent, x_sent, peer_sent, peer_got, up_sent, up_got,
):
    me = lax.axis_index("seq")
    blocks = kv_all.shape[0] // BLOCK
    levels = blocks // columns
    z = me // columns
    x = me % columns
    factor = WIDTH ** -0.5
    mesh_id = pl.DeviceIdType.MESH
    inner = z < levels - 1

    def rows_of(j):
        return pl.ds(pl.multiple_of(j * BLOCK, BLOCK), BLOCK)

    def beside(d):
        return lax.rem(x + d, columns)

    def before(d):
        return lax.rem(x + columns - d, columns)

    def z_copy(level):
        at = rows_of(level * columns + x)
        return pltpu.make_async_remote_copy(
            kv_all.at[at, :], kv_all.at[at, :], z_sent.at[level], got.at[level * columns + x],
            device_id={"seq": me + columns}, device_id_type=mesh_id,
        )

    def x_copy(level, d):
        at = rows_of(level * columns + x)
        return pltpu.make_async_remote_copy(
            kv_all.at[at, :], kv_all.at[at, :], x_sent.at[level, d - 1], got.at[level * columns + x],
            device_id={"seq": z * columns + beside(d)}, device_id_type=mesh_id,
        )

    def wait_block(j):
        at = rows_of(j)
        pltpu.make_async_copy(kv_all.at[at, :], kv_all.at[at, :], got.at[j]).wait()

    def peer_copy(level, d):
        return pltpu.make_async_remote_copy(
            peer_out.at[level, d - 1], peer_in.at[level, d - 1],
            peer_sent.at[level, d - 1], peer_got.at[level, d - 1],
            device_id={"seq": z * columns + beside(d)}, device_id_type=mesh_id,
        )

    def up_copy(level):
        return pltpu.make_async_remote_copy(
            up_out.at[level], up_in.at[level], up_sent.at[level], up_got.at[level],
            device_id={"seq": me - columns}, device_id_type=mesh_id,
        )

    def stats(j, first):
        keys = kv_all[rows_of(j), :WIDTH]
        values = kv_all[rows_of(j), WIDTH:]
        for g in range(HEADS):
            lanes = slice(g * WIDTH, (g + 1) * WIDTH)
            scores = dot(keys, q_ref[:, lanes], NT) * (factor * LOG2E)
            if first:
                scores = jnp.where(causal_mask(), scores, -jnp.inf)
            grads = dot(values, do_ref[:, lanes], NT)
            top = jnp.max(scores, axis=0, keepdims=True)
            shift = top
            if not first:
                old = peak[g]
                top = jnp.maximum(top + bias_ref[j], old)
                shift = top - bias_ref[j]
            terms = jnp.exp2(scores - shift)
            total = jnp.sum(terms, axis=0, keepdims=True)
            moved = jnp.sum(terms * grads, axis=0, keepdims=True)
            if not first:
                scale = jnp.exp2(old - top)
                total = total + mass[g] * scale
                moved = moved + weighted[g] * scale
            peak[g] = top
            mass[g] = total
            weighted[g] = moved

    def backward(j, first, store):
        keys = kv_all[rows_of(j), :WIDTH]
        values = kv_all[rows_of(j), WIDTH:]
        key_grad = jnp.zeros((BLOCK, WIDTH), jnp.float32)
        value_grad = jnp.zeros((BLOCK, WIDTH), jnp.float32)
        for g in range(HEADS):
            lanes = slice(g * WIDTH, (g + 1) * WIDTH)
            q = q_ref[:, lanes]
            do = do_ref[:, lanes]
            scores = dot(keys, q, NT) * (factor * LOG2E)
            shift = peak[g] if first else peak[g] - bias_ref[j]
            probs = jnp.exp2(scores - shift)
            if first:
                probs = jnp.where(causal_mask(), probs, 0.0)
            grads = dot(values, do, NT)
            dscores = (probs * ((grads - weighted[g]) * factor)).astype(jnp.bfloat16)
            value_grad = value_grad + dot(probs.astype(jnp.bfloat16), do, NN)
            key_grad = key_grad + dot(dscores, q, NN)
            dq_acc[:, lanes] += dot(dscores, keys, TN)
        store(slice(0, WIDTH), key_grad)
        store(slice(WIDTH, 2 * WIDTH), value_grad)

    kv_all[rows_of(me), :] = kv_ref[...]
    dq_acc[...] = jnp.zeros_like(dq_acc)
    barrier = pltpu.get_barrier_semaphore()
    for d in range(1, columns):
        pl.semaphore_signal(
            barrier, inc=1, device_id={"seq": z * columns + beside(d)}, device_id_type=mesh_id
        )

    @pl.when(inner)
    def _():
        pl.semaphore_signal(barrier, inc=1, device_id={"seq": me + columns}, device_id_type=mesh_id)

    @pl.when(z > 0)
    def _():
        pl.semaphore_signal(barrier, inc=1, device_id={"seq": me - columns}, device_id_type=mesh_id)

    pl.semaphore_wait(
        barrier, columns - 1 + jnp.where(inner, 1, 0) + jnp.where(z > 0, 1, 0)
    )

    @pl.when(inner)
    def _():
        z_copy(z).start()

    for d in range(1, columns):
        @pl.when(x + d < columns)
        def _():
            x_copy(z, d).start()

    stats(me, True)

    def stats_step(i, carry):
        level = z - 1 - i
        wait_block(level * columns + x)

        @pl.when(inner)
        def _():
            z_copy(level).start()

        for d in range(1, columns):
            x_copy(level, d).start()
        stats(level * columns + x, False)

        def one(d, inner_carry):
            j = level * columns + before(d)
            wait_block(j)
            stats(j, False)
            return inner_carry

        return lax.fori_loop(1, columns, one, carry)

    def own_level(d, carry):
        wait_block(me - d)
        stats(me - d, False)
        return carry

    lax.fori_loop(1, x + 1, own_level, 0)
    lax.fori_loop(0, z, stats_step, 0)
    for g in range(HEADS):
        weighted[g] = weighted[g] / mass[g]
        peak[g] = peak[g] + jnp.log2(mass[g])

    def store_col(level):
        def store(lanes, value):
            col[level, :, lanes] = value

        return store

    def send_peer(level, d):
        def store(lanes, value):
            peer_out[level, d - 1, :, lanes] = value.astype(jnp.bfloat16)

        backward(level * columns + beside(d), False, store)
        peer_copy(level, d).start()

    def add_up(level):
        @pl.when(inner)
        def _():
            up_copy(level).wait_recv()
            col[level] += up_in[level].astype(jnp.float32)

    def combine(level):
        for d in range(1, columns):
            peer_copy(level, d).wait_recv()
            col[level] += peer_in[level, d - 1].astype(jnp.float32)
        add_up(level)
        up_out[level] = col[level].astype(jnp.bfloat16)
        up_copy(level).start()

    def grad_step(level, carry):
        def one(d, inner_carry):
            send_peer(level, d)
            return inner_carry

        lax.fori_loop(1, columns, one, 0)
        backward(level * columns + x, False, store_col(level))

        @pl.when(level > 0)
        def _():
            combine(level - 1)

        return carry

    lax.fori_loop(0, z, grad_step, 0)

    def own_peer(d, carry):
        send_peer(z, d)
        return carry

    lax.fori_loop(columns - x, columns, own_peer, 0)

    @pl.when(z > 0)
    def _():
        combine(z - 1)

    backward(me, True, store_col(z))
    dq_ref[...] = dq_acc[...].astype(jnp.bfloat16)
    for d in range(1, columns):
        @pl.when(d > x)
        def _():
            peer_copy(z, d).wait_recv()
            col[z] += peer_in[z, d - 1].astype(jnp.float32)

    add_up(z)
    dkv_ref[...] = col[z].astype(jnp.bfloat16)

    def drain(level, carry):
        @pl.when(inner)
        def _():
            z_copy(level).wait_send()

        @pl.when(level < z)
        def _():
            up_copy(level).wait_send()

        for d in range(1, columns):
            @pl.when((level < z) | (x + d < columns))
            def _():
                x_copy(level, d).wait_send()

            @pl.when((level < z) | (x + d >= columns))
            def _():
                peer_copy(level, d).wait_send()

        return carry

    lax.fori_loop(0, z + 1, drain, 0)


def attention(blocks, bias, q, do, kv):
    window = blocks * BLOCK
    levels = 4
    columns = blocks // levels
    vmem = pl.BlockSpec(memory_space=pltpu.VMEM)
    pairs = HEADS * BLOCK * BLOCK * 7
    pair = (BLOCK, 2 * WIDTH)
    bf16, f32, dma = jnp.bfloat16, jnp.float32, pltpu.SemaphoreType.DMA
    return pl.pallas_call(
        functools.partial(attention_kernel, columns),
        out_shape=(
            jax.ShapeDtypeStruct((BLOCK, HEADS * WIDTH), bf16),
            jax.ShapeDtypeStruct(pair, bf16),
        ),
        in_specs=[vmem, vmem, vmem, vmem],
        out_specs=(vmem, vmem),
        scratch_shapes=[
            pltpu.VMEM((window, 2 * WIDTH), bf16),
            pltpu.VMEM((BLOCK, HEADS * WIDTH), f32),
            pltpu.VMEM((HEADS, 1, BLOCK), f32),
            pltpu.VMEM((HEADS, 1, BLOCK), f32),
            pltpu.VMEM((HEADS, 1, BLOCK), f32),
            pltpu.VMEM((levels,) + pair, f32),
            pltpu.VMEM((levels, columns - 1) + pair, bf16),
            pltpu.VMEM((levels, columns - 1) + pair, bf16),
            pltpu.VMEM((levels,) + pair, bf16),
            pltpu.VMEM((levels,) + pair, bf16),
            dma((blocks,)),
            dma((levels,)),
            dma((levels, columns - 1)),
            dma((levels, columns - 1)),
            dma((levels, columns - 1)),
            dma((levels,)),
            dma((levels,)),
        ],
        compiler_params=pltpu.CompilerParams(
            collective_id=2, has_side_effects=True, vmem_limit_bytes=48 * 2**20
        ),
        cost_estimate=pl.CostEstimate(
            flops=7 * 2 * pairs * WIDTH, bytes_accessed=6 * 2**20, transcendentals=2 * pairs
        ),
        name="attention",
    )(bias, q, do, kv)


def project_kernel(
    size, chunks, dq_ref, dkv_ref, wq_ref, wk_ref, wv_ref, out_ref,
    rows_all, mixed, wide, weights, product, own, core_out, core_in, far_out, far_in,
    w_sem, core_send, core_recv, far_send, far_recv,
):
    me = lax.axis_index("kvh")
    layer = me // 2
    core = me % 2
    layers = size // 2
    rows = BLOCK // size
    width = wk_ref.shape[0] // chunks
    qw = HEADS * WIDTH
    peer = layer * 2 + 1 - core

    def weight_copies(i):
        at = pl.ds(pl.multiple_of(i * width, width), width)
        return [
            pltpu.make_async_copy(
                wq_ref.at[pl.ds(pl.multiple_of(i * width * HEADS, width * HEADS), width * HEADS), :],
                mixed.at[i], w_sem.at[i, 0],
            ),
            pltpu.make_async_copy(wk_ref.at[at, :], weights.at[i, :, pl.ds(qw, WIDTH)], w_sem.at[i, 1]),
            pltpu.make_async_copy(
                wv_ref.at[at, :], weights.at[i, :, pl.ds(qw + WIDTH, WIDTH)], w_sem.at[i, 2]
            ),
        ]

    def start_weights(i, carry):
        for copy in weight_copies(i):
            copy.start()
        return carry

    lax.fori_loop(0, chunks, start_weights, 0)
    barrier = pltpu.get_barrier_semaphore()
    far = [lax.rem(layer + d, layers) for d in range(layers)]
    pl.semaphore_signal(barrier, inc=1, device_id={"kvh": peer}, device_id_type=pl.DeviceIdType.MESH)
    for d in range(1, layers):
        pl.semaphore_signal(
            barrier, inc=1, device_id={"kvh": far[d] * 2 + core}, device_id_type=pl.DeviceIdType.MESH
        )
    rows_all[:, :qw] = dq_ref[...]
    rows_all[:, qw:] = dkv_ref[...]
    pl.semaphore_wait(barrier, layers)

    def core_copy(d, i):
        return pltpu.make_async_remote_copy(
            core_out.at[d, i], core_in.at[d, i], core_send.at[d, i], core_recv.at[d, i],
            device_id={"kvh": peer}, device_id_type=pl.DeviceIdType.MESH,
        )

    def far_copy(d, i):
        return pltpu.make_async_remote_copy(
            far_out.at[d - 1, i], far_in.at[d - 1, i], far_send.at[d - 1, i], far_recv.at[d - 1, i],
            device_id={"kvh": far[d] * 2 + core}, device_id_type=pl.DeviceIdType.MESH,
        )

    def part(d, which):
        return pl.ds(pl.multiple_of((far[d] * 2 + which) * rows, rows), rows)

    def begin(i):
        for copy in weight_copies(i):
            copy.wait()
        slot = i % 2
        wide[...] = mixed[i].astype(jnp.float32)
        for g in range(HEADS):
            weights[i, :, g * WIDTH:(g + 1) * WIDTH] = wide[pl.ds(g, width, HEADS), :].astype(jnp.bfloat16)
        product[slot] = dot(rows_all[...], weights[i], NT)
        for d in list(range(1, layers)) + [0]:
            core_out[d, i] = product[slot, part(d, 1 - core), :].astype(jnp.bfloat16)
            core_copy(d, i).start()

    def forward(i):
        slot = i % 2
        for d in range(1, layers):
            core_copy(d, i).wait_recv()
            far_out[d - 1, i] = (
                product[slot, part(d, core), :] + core_in[d, i].astype(jnp.float32)
            ).astype(jnp.bfloat16)
            far_copy(d, i).start()
        own[i] = product[slot, part(0, core), :]

    begin(0)

    def step(i, carry):
        begin(i)
        forward(i - 1)
        return carry

    lax.fori_loop(1, chunks, step, 0)
    forward(chunks - 1)

    def finish(i, carry):
        core_copy(0, i).wait_recv()
        total = own[i] + core_in[0, i].astype(jnp.float32)
        for d in range(1, layers):
            far_copy(d, i).wait_recv()
            total = total + far_in[d - 1, i].astype(jnp.float32)
        out_ref[:, pl.ds(pl.multiple_of(i * width, width), width)] = total.astype(jnp.bfloat16)
        for d in range(layers):
            core_copy(d, i).wait_send()
        for d in range(1, layers):
            far_copy(d, i).wait_send()
        return carry

    lax.fori_loop(0, chunks, finish, 0)


def project(size, dq, dkv, wq, wk, wv):
    model = wk.shape[0]
    rows = BLOCK // size
    layers = size // 2
    chunks = 16
    width = model // chunks
    vmem = pl.BlockSpec(memory_space=pltpu.VMEM)
    hbm = pl.BlockSpec(memory_space=pl.ANY)
    full = (HEADS + 2) * WIDTH
    return pl.pallas_call(
        functools.partial(project_kernel, size, chunks),
        out_shape=jax.ShapeDtypeStruct((rows, model), jnp.bfloat16),
        in_specs=[vmem, vmem, hbm, hbm, hbm],
        out_specs=vmem,
        scratch_shapes=[
            pltpu.VMEM((BLOCK, full), jnp.bfloat16),
            pltpu.VMEM((chunks, width * HEADS, WIDTH), jnp.bfloat16),
            pltpu.VMEM((width * HEADS, WIDTH), jnp.float32),
            pltpu.VMEM((chunks, width, full), jnp.bfloat16),
            pltpu.VMEM((2, BLOCK, width), jnp.float32),
            pltpu.VMEM((chunks, rows, width), jnp.float32),
            pltpu.VMEM((layers, chunks, rows, width), jnp.bfloat16),
            pltpu.VMEM((layers, chunks, rows, width), jnp.bfloat16),
            pltpu.VMEM((layers - 1, chunks, rows, width), jnp.bfloat16),
            pltpu.VMEM((layers - 1, chunks, rows, width), jnp.bfloat16),
            pltpu.SemaphoreType.DMA((chunks, 3)),
            pltpu.SemaphoreType.DMA((layers, chunks)),
            pltpu.SemaphoreType.DMA((layers, chunks)),
            pltpu.SemaphoreType.DMA((layers - 1, chunks)),
            pltpu.SemaphoreType.DMA((layers - 1, chunks)),
        ],
        compiler_params=pltpu.CompilerParams(
            collective_id=1, has_side_effects=True, vmem_limit_bytes=56 * 2**20
        ),
        cost_estimate=pl.CostEstimate(
            flops=2 * BLOCK * full * model, bytes_accessed=2 * full * model, transcendentals=0
        ),
        name="project",
    )(dq, dkv, wq, wk, wv)


def local(
    size, queries, key_states, value_states, grad_out, ancestors, query_weight, key_weight, value_weight
):
    model = query_weight.shape[0]
    q = queries.reshape(BLOCK, HEADS * WIDTH)
    do = grad_out.reshape(BLOCK, HEADS * WIDTH)
    kv = jnp.concatenate([key_states[:, 0], value_states[:, 0]], 1)
    blocks = ancestors.shape[0]
    me = lax.axis_index("seq")
    listed = lax.dynamic_index_in_dim(ancestors, me, 0, keepdims=False)
    ids = jnp.arange(blocks, dtype=jnp.int32)
    visible = jnp.any(listed[None, :] == ids[:, None], axis=1)
    bias = jnp.where(visible, 0.0, -jnp.inf).astype(jnp.float32)
    bias = jnp.broadcast_to(bias[:, None, None], (blocks, 1, BLOCK))
    dq, pair = attention(blocks, bias, q, do, kv)
    grad_input = project(
        size, dq, pair,
        query_weight.reshape(model * HEADS, WIDTH), key_weight[:, 0], value_weight[:, 0],
    )
    return (grad_input, pair[:, None, :WIDTH], pair[:, None, WIDTH:])


def solution(mesh):
    return jax.shard_map(
        functools.partial(local, mesh.shape["kvh"]),
        mesh=mesh,
        in_specs=(
            P("seq", "kvh", None, None),
            P("seq", "kvh", None),
            P("seq", "kvh", None),
            P("seq", "kvh", None, None),
            P(),
            P(None, "kvh", None, None),
            P(None, "kvh", None),
            P(None, "kvh", None),
        ),
        out_specs=(P(("seq", "kvh"), None), P("seq", "kvh", None), P("seq", "kvh", None)),
        check_vma=False,
    )
```
